32 devices in a mesh: groups: 1, cells: 32 (over z, y, x, core).
Axes of the slice: x: 2, y: 2, z: 4, core: 2. Of those that a mesh axis runs over, the one named last changes fastest.
Arguments:
- expression: bfloat16 [49152, 3072], P(('groups', 'cells')), may hold values from 0.019897461 to 4
- dataset_ids: int32 [49152, 1], P(('groups', 'cells')), may hold values from 0 to 31; in each aligned block of 1536 rows (0 to 1535, 1536 to 3071, ...) at most 64 rows name the same one
- owner_map: int32 [32], P('groups'), may hold values from 0 to 31, each once
- atlas_sizes: int32 [32], P('groups'), may hold values from 16384 to 131071
- loadings: bfloat16 [64, 49152], P(None, ('groups', 'cells')), may hold values from 0.049804688 to 1
- shared: float32 [64, 3072], P('groups'), may hold values from 0 to 0.5
- specific: float32 [32, 64, 3072], P(('groups', 'cells')), may hold values from 0 to 0.2
Outputs:
- loadings_out: float32 [64, 49152], P(None, ('groups', 'cells'))
- shared_out: float32 [64, 3072], P('groups')
- specific_out: float32 [32, 64, 3072], P(('groups', 'cells'))
The draws below stay inside these ranges and needn't reach their ends.
Inputs may be any that keep to these rules, and one draw needn't show every extreme that they name: `dataset_ids`: among the cells of one device at most 64 belong to one dataset, and exactly 64 do in some dataset; every dataset has cells in the window. `owner_map`: each device owns exactly one dataset.
All inputs are finite; a program needn't handle non-finite values. Where the reference program divides by a largest or mean magnitude, that divisor is 1e-20 or more.
Results may differ from the reference program's by a relative error of at most 0.0003.
Values may be sent and summed in bfloat16 or wider, within the bound.
A program may use at most 192 MiB of HBM per device.

```python
import math
import jax
import jax.numpy as jnp
import numpy as np
from jax import lax

GENES = 3072
FACTORS = 64
CELLS_DEV = 1536
SLOTS = 64
PASSES = 3
DATASETS = 32
CELLS = 49152
N_CELLS = 32


def with_ends(result, own_key, low, high):
    dims = result.shape
    index_at = [jax.random.randint(jax.random.fold_in(own_key, axis), (), 0, dims[axis]) for axis in range(len(dims))]
    result = result.at[tuple(index_at)].set(low)
    longest = dims.index(max(dims))
    index_at[longest] = (index_at[longest] + 1) % dims[longest]
    return result.at[tuple(index_at)].set(high)


def steps_of(stream_key, extent, shards, least, high):
    def one(dim, parts):
        draws = jax.random.uniform(jax.random.fold_in(jax.random.fold_in(stream_key, 6), dim), (parts,), jnp.float32, least / len(shards), high / len(shards))
        return jnp.repeat(jnp.exp(draws), extent[dim] // parts).reshape((-1,) + (1,) * (len(extent) - dim - 1))

    factor_of = one(*shards[0])
    for cut in shards[1:]:
        factor_of = factor_of * one(*cut)
    return factor_of


def assign_block(own_key, own, number, rows, amount, top, most, skew):
    sequence = jax.random.permutation(own_key, amount)
    crowded, usual = shares(amount, rows * top, most, skew, True), shares(amount, rows * top, most, skew, False)
    places = jnp.arange(amount)

    def named(tallies, offset_by):
        used = int((tallies > 0).sum())
        fixed = max(1, used // 4)
        shifted = fixed + (places - fixed + offset_by * (used - fixed)) % max(1, amount - fixed)
        return jnp.zeros((amount,), jnp.int32).at[sequence[jnp.where(places < fixed, places, shifted)]].set(jnp.asarray(tallies, jnp.int32))

    tallies = jnp.where(number % 4 == 0, named(crowded, number // 4), named(usual, number - number // 4 - 1))
    mixed = jax.random.permutation(jax.random.fold_in(own, 3), amount)
    source_of, sink = mixed[0:amount // 2 * 2:2], mixed[1:amount // 2 * 2:2]
    margin = jnp.minimum(tallies[source_of] - 1, most - tallies[sink]) // 2
    margin = jnp.where((source_of == sequence[0]) | (sink == sequence[0]) | (tallies[sink] == 0), 0, jnp.maximum(margin, 0))
    shifted = jax.random.randint(jax.random.fold_in(own, 4), (amount // 2,), 0, 1 << 20) % (margin + 1)
    tallies = tallies.at[source_of].add(-shifted).at[sink].add(shifted)
    items = jnp.searchsorted(jnp.cumsum(tallies), jnp.arange(rows * top), side="right").astype(jnp.int32)
    table = items.reshape(top, rows).T
    table = table[jax.random.permutation(jax.random.fold_in(own, 1), rows)]
    offset_by = jax.random.randint(jax.random.fold_in(own, 2), (rows, 1), 0, top)
    return jnp.take_along_axis(table, (jnp.arange(top)[None, :] + offset_by) % top, axis=1)


def shares(number_of, total, most, lean, full):
    portions = [(1 << 20) // math.isqrt(standing ** lean) + 1 for standing in range(1, number_of + 1)]
    largest = most if full else min(most, max(-(-total // number_of), total * portions[0] // sum(portions)))
    least = 1 if total - largest >= number_of - 1 else 0
    holding, rest = [largest] + [least] * (number_of - 1), total - largest - least * (number_of - 1)
    while rest > 0:
        free = [i for i in range(1, number_of) if holding[i] < largest] or [i for i in range(1, number_of) if holding[i] < most]
        mass, budget = sum([portions[i] for i in free]), rest
        for i in free:
            addition = min(most - holding[i], max(1, budget * portions[i] // mass), rest)
            holding[i] = holding[i] + addition
            rest = rest - addition
    return np.array(holding)


def setup_inputs(seed: int = 0, part: int = 0) -> dict:
    seeds = jax.random.split(jax.random.key(seed), 8)
    part_keys = jax.random.split(jax.random.fold_in(seeds[7], part), 8)
    expression = jnp.clip(jnp.exp(math.log(4.0) - 5.3034575 * jax.random.uniform(part_keys[0], (CELLS, GENES), jnp.float32) ** steps_of(part_keys[0], (CELLS, GENES), ((0, 32),), -0.2, 0.2)), 0.019897461, 4.0).astype(jnp.bfloat16)
    dataset_ids_keys = jax.random.split(jax.random.fold_in(part_keys[1], 1), CELLS // CELLS_DEV)
    dataset_ids_turns = jax.random.permutation(jax.random.fold_in(part_keys[1], 3), CELLS // CELLS_DEV)
    dataset_ids = jax.vmap(lambda own, number: assign_block(jax.random.fold_in(part_keys[1], 2), own, number, CELLS_DEV, DATASETS, 1, SLOTS, 2))(dataset_ids_keys, dataset_ids_turns).reshape((CELLS, 1))
    owner_map = jax.random.permutation(part_keys[2], DATASETS).astype(jnp.int32)
    atlas_sizes = with_ends(jax.random.randint(part_keys[3], (DATASETS,), 16384, 131072), jax.random.fold_in(part_keys[3], 1), 16384, 131071).astype(jnp.int32)
    loadings = jnp.clip(0.049804688 + 0.9501953 * jax.random.uniform(part_keys[4], (FACTORS, CELLS), jnp.float32) ** steps_of(part_keys[4], (FACTORS, CELLS), ((1, 32),), -0.2, 0.2), 0.049804688, 1.0).astype(jnp.bfloat16)
    shared = jnp.clip(jax.random.uniform(part_keys[5], (FACTORS, GENES), jnp.float32, 0.0, 0.5), 0.0, 0.5)
    specific = jnp.clip(0.2 * jax.random.uniform(part_keys[6], (DATASETS, FACTORS, GENES), jnp.float32) ** steps_of(part_keys[6], (DATASETS, FACTORS, GENES), ((0, 32),), -0.2, 0.2), 0.0, 0.2)
    return dict(expression=expression, dataset_ids=dataset_ids, owner_map=owner_map, atlas_sizes=atlas_sizes, loadings=loadings, shared=shared, specific=specific)


penalty = 5.0


def rounded(values):
    low = lax.optimization_barrier(values.astype(jnp.bfloat16))
    return low.astype(jnp.float32)


def hdot(left, right):
    return jnp.dot(left, right, preferred_element_type=jnp.float32, precision=lax.Precision.HIGHEST)


def reference(expression, dataset_ids, owner_map, atlas_sizes, loadings, shared, specific):
    row_total = N_CELLS * SLOTS
    target = owner_map[dataset_ids[:, 0]].astype(jnp.int32)

    def per_owner(owner):
        member = target == owner
        member_count = jnp.sum(member.astype(jnp.int32))
        count = member_count.astype(jnp.float32)
        index_list = jnp.nonzero(member, size=row_total, fill_value=0)[0].astype(jnp.int32)
        valid = (jnp.arange(row_total) < member_count).astype(jnp.float32)
        rows = expression[index_list].astype(jnp.float32) * valid[:, None]
        loading = loadings[:, index_list].astype(jnp.float32) * valid[None, :]
        own_specific = specific[owner]
        factor = shared + own_specific
        projected = hdot(rounded(factor), rows.T)
        curvature = hdot(factor, factor.T) + penalty * hdot(own_specific, own_specific.T)
        step_size = 1.0 / jnp.max(jnp.sum(jnp.abs(curvature), axis=1))
        for turn in range(PASSES):
            loading = jnp.maximum(loading - step_size * (hdot(curvature, loading) - projected), 0.0)
        gram_stat = hdot(loading, loading.T) / count
        cross_stat = hdot(rounded(loading), rows) / count
        weight_own = jnp.sum(jnp.where(owner_map == owner, atlas_sizes, 0)).astype(jnp.float32) / 65536.0
        gradient = hdot(gram_stat, factor) - cross_stat
        row_bound = jnp.max(jnp.sum(gram_stat, axis=1))
        new_specific = jnp.maximum(own_specific - (gradient + penalty * hdot(gram_stat, own_specific)) / ((1.0 + penalty) * row_bound + 1e-6), 0.0)
        return loading, index_list, valid, weight_own * gradient, weight_own * row_bound, new_specific

    owners = jnp.arange(N_CELLS, dtype=jnp.int32)
    loads, index_all, valid_all, grad_terms, bound_terms, specific_out = lax.map(per_owner, owners)
    masked = (loads * valid_all[:, None, :]).transpose(1, 0, 2).reshape(FACTORS, -1)
    loadings_out = jnp.zeros(loadings.shape, jnp.float32).at[:, index_all.reshape(-1)].add(masked)
    shared_out = jnp.maximum(shared - jnp.sum(grad_terms, axis=0) / jnp.sum(bound_terms), 0.0)
    return loadings_out, shared_out, specific_out
```

```python
import jax
import jax.numpy as jnp
from jax import lax
from jax.sharding import PartitionSpec as P

PASSES = 3
PENALTY = 5.0


def hdot(left, right):
    return jnp.dot(left, right, preferred_element_type=jnp.float32, precision=lax.Precision.HIGHEST)


def split(x):
    high = lax.reduce_precision(x, 8, 7)
    return high.astype(jnp.bfloat16), (x - high).astype(jnp.bfloat16)


def body(expression, dataset_ids, owner_map, atlas_sizes, loadings, shared, specific):
    owners = lax.axis_size("cells")
    me = lax.axis_index("cells")
    cells, genes = expression.shape
    factors = shared.shape[0]
    v = specific[0]
    q = shared + v
    qb_all = lax.all_gather(q.astype(jnp.bfloat16), "cells", axis=0, tiled=True)
    curvature = hdot(q, q.T) + PENALTY * hdot(v, v.T)
    step = 1.0 / jnp.max(jnp.sum(jnp.abs(curvature), axis=1))
    small = jnp.concatenate([curvature * step, jnp.full((factors, factors), step)], axis=1)
    small_all = lax.all_gather(small, "cells", axis=0, tiled=True)
    ids = dataset_ids[:, 0]
    chosen = ids[:, None] == jnp.arange(owner_map.shape[0], dtype=jnp.int32)[None, :]
    target = jnp.sum(jnp.where(chosen, owner_map[None, :], 0), axis=1)
    mask = target[None, :] == jnp.arange(owners, dtype=jnp.int32)[:, None]
    count_all = lax.psum(jnp.sum(mask.astype(jnp.float32), axis=1), "cells")

    def pick(stacked):
        return jnp.sum(
            jnp.where(mask[:, None, :], stacked.reshape(owners, factors, cells), 0.0), axis=0
        )

    m_high, m_low = split(small_all[:, :factors])
    m_cat = jnp.concatenate([m_high, m_low, m_high], axis=1)
    steps = small_all.reshape(owners, factors, 2 * factors)[:, 0, factors]
    cell_step = jnp.sum(jnp.where(mask, steps[:, None], 0.0), axis=0)
    projected = pick(
        lax.dot_general(
            qb_all, expression, (((1,), (1,)), ((), ())), preferred_element_type=jnp.float32
        )
    )
    pull = projected * cell_step[None, :]
    h = loadings.astype(jnp.float32)
    for _ in range(PASSES):
        high, low = split(h)
        h_cat = jnp.concatenate([high, high, low], axis=0)
        applied = pick(jnp.dot(m_cat, h_cat, preferred_element_type=jnp.float32))
        h = jnp.maximum(h - applied + pull, 0.0)
    high, low = split(h)
    masked = jnp.where(mask[:, None, :], high[None], jnp.bfloat16(0)).reshape(
        owners * factors, cells
    )
    gram_part = jnp.dot(
        masked, jnp.concatenate([high.T, low.T], axis=1), preferred_element_type=jnp.float32
    )
    cross_part = jnp.dot(masked, expression, preferred_element_type=jnp.float32)
    gram2 = lax.psum_scatter(gram_part, "cells", scatter_dimension=0, tiled=True)
    cross = lax.psum_scatter(cross_part, "cells", scatter_dimension=0, tiled=True)
    count = jnp.sum(jnp.where(jnp.arange(owners) == me, count_all, 0.0))
    mixed = gram2[:, factors:]
    gram = (gram2[:, :factors] + mixed + mixed.T) / count
    weight = jnp.sum(jnp.where(owner_map == me, atlas_sizes, 0)).astype(jnp.float32) / 65536.0
    gradient = hdot(gram, q) - cross / count
    bound = jnp.max(jnp.sum(gram, axis=1))
    new_specific = jnp.maximum(
        v - (gradient + PENALTY * hdot(gram, v)) / ((1.0 + PENALTY) * bound + 1e-06), 0.0
    )
    grad_total, bound_total = lax.psum((weight * gradient, weight * bound), "cells")
    shared_out = jnp.maximum(shared - grad_total / bound_total, 0.0)
    return (h, shared_out, new_specific[None])


def solution(mesh):
    placed = (
        P(("groups", "cells"), None),
        P(("groups", "cells"), None),
        P("groups"),
        P("groups"),
        P(None, ("groups", "cells")),
        P("groups", None),
        P(("groups", "cells"), None, None),
    )
    return jax.shard_map(
        body,
        mesh=mesh,
        in_specs=placed,
        out_specs=(
            P(None, ("groups", "cells")),
            P("groups", None),
            P(("groups", "cells"), None, None),
        ),
        check_vma=False,
    )
```

```python
import functools

import jax
import jax.numpy as jnp
from jax import lax
from jax.experimental import pallas as pl
from jax.experimental.pallas import tpu as pltpu
from jax.sharding import PartitionSpec as P

PASSES = 3
PENALTY = 5.0
PARTS = 3
GROUP = 4
VMEM = 127 * 512 * 1024


def hdot(left, right):
    return jnp.dot(left, right, preferred_element_type=jnp.float32, precision=lax.Precision.HIGHEST)


def nt_dot(left, right):
    return lax.dot_general(
        left, right, (((1,), (1,)), ((), ())), preferred_element_type=jnp.float32
    )


def orders_of(devices):
    high = []
    bit = devices // 2
    while bit > 1:
        high.append(bit)
        bit //= 2
    rolls = [0, len(high) - 1, len(high) // 2]
    orders = [high[k:] + high[:k] + [1] for k in rolls]
    return orders + [orders[0]]


def flip(me, bits):
    for bit in bits:
        me = me + bit - 2 * bit * ((me // bit) % 2)
    return me


def slots_of(target, me, order):
    apart = jnp.bitwise_xor(target, me)
    return sum(((apart // bit) % 2) * (1 << j) for j, bit in enumerate(order))


def enter(me, devices):
    barrier = pltpu.get_barrier_semaphore()
    bit = 1
    count = 0
    while bit < devices:
        pl.semaphore_signal(
            barrier,
            inc=1,
            device_id={"cells": flip(me, [bit])},
            device_id_type=pl.DeviceIdType.MESH,
        )
        bit *= 2
        count += 1
    pl.semaphore_wait(barrier, count)


def exchange(source, landing, sends, receives, part, stage, me, bit):
    return pltpu.make_async_remote_copy(
        src_ref=source,
        dst_ref=landing,
        send_sem=sends.at[part, stage],
        recv_sem=receives.at[part, stage],
        device_id={"cells": flip(me, [bit])},
        device_id_type=pl.DeviceIdType.MESH,
    )


def load_kernel(
    devices, q_ref, small_ref, x_ref, rel_ref, start_ref, h_ref, mean_ref, buf, side, acc, steps, sends, recvs
):
    me = lax.axis_index("cells")
    orders = orders_of(devices)
    stages = len(orders[0])
    factors, genes = q_ref.shape
    cells = x_ref.shape[0]
    width = genes // PARTS
    rows = GROUP * factors
    for p in range(PARTS):
        buf[p, 0] = q_ref[:, p * width : (p + 1) * width]
    side[0] = small_ref[...]
    acc[...] = jnp.zeros_like(acc)
    enter(me, devices)

    def copy(p, j):
        near, far = pl.ds(0, 1 << j), pl.ds(1 << j, 1 << j)
        if p == PARTS:
            return exchange(side.at[near], side.at[far], sends, recvs, p, j, me, orders[p][j])
        return exchange(buf.at[p, near], buf.at[p, far], sends, recvs, p, j, me, orders[p][j])

    def project(low, high):
        for p in range(PARTS):

            def one(g, carry, p=p):
                block = buf[p, pl.ds(g * GROUP, GROUP)].reshape(rows, width)
                product = nt_dot(block, x_ref[:, p * width : (p + 1) * width])
                slot = rel_ref[p : p + 1, :]
                total = acc[...]
                for i in range(GROUP):
                    total = total + jnp.where(
                        slot == g * GROUP + i, product[i * factors : (i + 1) * factors], 0.0
                    )
                acc[...] = total
                return carry

            lax.fori_loop(low // GROUP, high // GROUP, one, 0)

    for p in range(PARTS + 1):
        copy(p, 0).start()
    for j in range(stages):
        for p in range(PARTS + 1):
            copy(p, j).wait()
            if j + 1 < stages:
                copy(p, j + 1).start()
        if j == 1:
            project(0, 4)
        elif j > 1:
            project(1 << j, 2 << j)

    slot = rel_ref[PARTS : PARTS + 1, :]

    def step_of(s, carry):
        one = side[s][factors - 1 : factors, factors : factors + 1]
        mean_ref[...] = mean_ref[...] + side[s] * (1.0 / devices)
        steps[...] = steps[...] + jnp.where(slot == s, one, 0.0)
        return carry

    steps[...] = jnp.zeros_like(steps)
    mean_ref[...] = jnp.zeros_like(mean_ref)
    lax.fori_loop(0, devices, step_of, 0)
    acc[...] = acc[...] * steps[...]
    h_ref[...] = start_ref[...].astype(jnp.float32)
    for _ in range(PASSES):
        h = h_ref[...]
        high = h.astype(jnp.bfloat16)
        low = (h - high.astype(jnp.float32)).astype(jnp.bfloat16)
        h_cat = jnp.concatenate([high, high, low], axis=0)
        h_ref[...] = h + acc[...]

        def apply(g, carry, h_cat=h_cat):
            m = side[pl.ds(g * GROUP, GROUP)].reshape(rows, 2 * factors)[:, :factors]
            m_high = m.astype(jnp.bfloat16)
            m_low = (m - m_high.astype(jnp.float32)).astype(jnp.bfloat16)
            m_cat = jnp.concatenate([m_high, m_low, m_high], axis=1)
            product = jnp.dot(m_cat, h_cat, preferred_element_type=jnp.float32)
            total = h_ref[...]
            for i in range(GROUP):
                total = total - jnp.where(
                    slot == g * GROUP + i, product[i * factors : (i + 1) * factors], 0.0
                )
            h_ref[...] = total
            return carry

        lax.fori_loop(0, devices // GROUP, apply, 0)
        h_ref[...] = jnp.maximum(h_ref[...], 0.0)


def stat_kernel(
    devices, h_ref, x_ref, rel_ref, mean_ref, cross_ref, gram_ref, buf, land, side, side_land, held, arrived,
    sends, recvs
):
    me = lax.axis_index("cells")
    orders = orders_of(devices)
    stages = len(orders[0])
    factors, cells = h_ref.shape
    genes = x_ref.shape[1]
    width = genes // PARTS
    group = GROUP if devices <= 32 else GROUP // 2
    streamed = devices > 32
    enter(me, devices)

    def copy(p, j):
        far, landed = pl.ds(1 << j, 1 << j), pl.ds((1 << j) - 1, 1 << j)
        if p == PARTS:
            return exchange(side.at[far], side_land.at[landed], sends, recvs, p, j, me, orders[p][j])
        return exchange(buf.at[p, far], land.at[p, landed], sends, recvs, p, j, me, orders[p][j])

    def masked(p, g):
        slot = rel_ref[p : p + 1, :]
        h = h_ref[...]
        return jnp.concatenate(
            [jnp.where(slot == g * group + i, h, 0.0).astype(jnp.bfloat16) for i in range(group)],
            axis=0,
        )

    def fill(p, low, high):
        if streamed:
            fetch = pltpu.make_async_copy(x_ref.at[:, pl.ds(p * width, width)], held, arrived)
            fetch.start()
            fetch.wait()

        def one(g, carry):
            load = masked(p, g)
            columns = held[...] if streamed else x_ref[:, p * width : (p + 1) * width]
            product = jnp.dot(load, columns, preferred_element_type=jnp.float32)
            mass = jnp.sum(load.astype(jnp.float32), axis=1, keepdims=True)
            product = product - mass * mean_ref[:, p * width : (p + 1) * width]
            buf[p, pl.ds(g * group, group)] = product.astype(jnp.bfloat16).reshape(
                group, factors, width
            )
            return carry

        lax.fori_loop(low // group, high // group, one, 0)

    def fill_side(low, high):
        h = h_ref[...]
        h_high = h.astype(jnp.bfloat16)
        h_low = (h - h_high.astype(jnp.float32)).astype(jnp.bfloat16)
        both = jnp.concatenate([h_high, h_low], axis=0)
        slot = rel_ref[PARTS : PARTS + 1, :]

        def one(g, carry):
            load = masked(PARTS, g)
            product = nt_dot(load, both)
            mass = nt_dot(jnp.ones((16, cells), jnp.bfloat16), load)[0:8]
            for i in range(group):
                s = g * group + i
                here = jnp.sum(jnp.where(slot == s, 1.0, 0.0), axis=1, keepdims=True)
                side[s, 0:factors, :] = product[i * factors : (i + 1) * factors]
                side[s, factors : factors + 8, :] = jnp.concatenate(
                    [
                        mass[:, i * factors : (i + 1) * factors],
                        jnp.broadcast_to(here, (8, factors)),
                    ],
                    axis=1,
                )
            return carry

        lax.fori_loop(low // group, high // group, one, 0)

    def gather_in(p, j, low, high):
        def one(s, carry):
            if p == PARTS:
                side[s] = side[s] + side_land[(1 << j) - 1 + s]
            else:
                buf[p, s] = (
                    buf[p, s].astype(jnp.float32) + land[p, (1 << j) - 1 + s].astype(jnp.float32)
                ).astype(jnp.bfloat16)
            return carry

        lax.fori_loop(low, high, one, 0)

    half = devices // 2
    for p in range(PARTS):
        fill(p, half, devices)
        copy(p, stages - 1).start()
    fill_side(half, devices)
    copy(PARTS, stages - 1).start()
    for p in range(PARTS):
        fill(p, 0, half)
    fill_side(0, half)
    for j in range(stages - 1, 0, -1):
        for p in range(PARTS + 1):
            copy(p, j).wait()
            gather_in(p, j, 1 << (j - 1), 1 << j)
            copy(p, j - 1).start()
        for p in range(PARTS + 1):
            gather_in(p, j, 0, 1 << (j - 1))
    for p in range(PARTS):
        copy(p, 0).wait()
        cross_ref[:, p * width : (p + 1) * width] = buf[p, 0].astype(jnp.float32) + land[
            p, 0
        ].astype(jnp.float32)
    copy(PARTS, 0).wait()
    gram_ref[...] = side[0] + side_land[0]


def sum_kernel(devices, x_ref, out_ref, buf, land, spread, sends, recvs):
    me = lax.axis_index("cells")
    order = orders_of(devices)[0]
    stages = len(order)

    def block(r):
        return flip(me, [bit for j, bit in enumerate(order) if (r >> j) % 2])

    for r in range(devices):
        buf[r] = x_ref[block(r)]
    enter(me, devices)

    def inward(j):
        far = pl.ds(1 << j, 1 << j)
        return exchange(buf.at[far], land.at[far], sends, recvs, 0, j, me, order[j])

    def outward(j):
        near, far = pl.ds(0, 1 << j), pl.ds(1 << j, 1 << j)
        return exchange(spread.at[near], spread.at[far], sends, recvs, 1, j, me, order[j])

    for j in range(stages - 1, -1, -1):
        inward(j).start()
        inward(j).wait()
        near = pl.ds(0, 1 << j)
        buf[near] = buf[near] + land[pl.ds(1 << j, 1 << j)]
    spread[0] = buf[0]
    for j in range(stages):
        outward(j).start()
        outward(j).wait()
    for r in range(devices):
        out_ref[block(r)] = spread[r]


def in_vmem(count):
    return [pl.BlockSpec(memory_space=pltpu.VMEM)] * count


def params(number):
    return pltpu.CompilerParams(
        collective_id=number, has_side_effects=True, vmem_limit_bytes=VMEM
    )


def body(expression, dataset_ids, owner_map, atlas_sizes, loadings, shared, specific):
    devices = lax.axis_size("cells")
    me = lax.axis_index("cells")
    cells, genes = expression.shape
    factors = shared.shape[0]
    width = genes // PARTS
    orders = orders_of(devices)
    stages = len(orders[0])
    v = specific[0]
    q = shared + v
    curvature = hdot(q, q.T) + PENALTY * hdot(v, v.T)
    step = 1.0 / jnp.max(jnp.sum(jnp.abs(curvature), axis=1))
    lines = genes // factors
    typical = jnp.mean(expression[: cells // 6].astype(jnp.float32), axis=0)
    extra = jnp.concatenate(
        [typical.reshape(lines, factors), jnp.full((factors - lines, factors), step)], axis=0
    )
    small = jnp.concatenate([curvature * step, extra], axis=1)
    ids = dataset_ids[:, 0]
    chosen = ids[None, :] == jnp.arange(owner_map.shape[0], dtype=jnp.int32)[:, None]
    target = jnp.sum(jnp.where(chosen, owner_map[:, None], 0), axis=0)
    rel = jnp.stack([slots_of(target, me, order) for order in orders] * 2, axis=0)
    semaphores = [
        pltpu.SemaphoreType.DMA((PARTS + 1, stages)),
        pltpu.SemaphoreType.DMA((PARTS + 1, stages)),
    ]
    h, mean = pl.pallas_call(
        functools.partial(load_kernel, devices),
        out_shape=(
            jax.ShapeDtypeStruct((factors, cells), jnp.float32),
            jax.ShapeDtypeStruct((factors, 2 * factors), jnp.float32),
        ),
        in_specs=in_vmem(5),
        out_specs=tuple(in_vmem(2)),
        scratch_shapes=[
            pltpu.VMEM((PARTS, devices, factors, width), jnp.bfloat16),
            pltpu.VMEM((devices, factors, 2 * factors), jnp.float32),
            pltpu.VMEM((factors, cells), jnp.float32),
            pltpu.VMEM((1, cells), jnp.float32),
        ]
        + semaphores,
        compiler_params=params(0),
        name="load_kernel",
    )(q.astype(jnp.bfloat16), small, expression, rel, loadings)
    center = mean[:lines, factors:].reshape(1, genes)
    cross, gram2 = pl.pallas_call(
        functools.partial(stat_kernel, devices),
        out_shape=(
            jax.ShapeDtypeStruct((factors, genes), jnp.float32),
            jax.ShapeDtypeStruct((factors + 8, 2 * factors), jnp.float32),
        ),
        in_specs=in_vmem(1)
        + [pl.BlockSpec(memory_space=pl.ANY if devices > 32 else pltpu.VMEM)]
        + in_vmem(2),
        out_specs=tuple(in_vmem(2)),
        scratch_shapes=[
            pltpu.VMEM((PARTS, devices, factors, width), jnp.bfloat16),
            pltpu.VMEM((PARTS, devices - 1, factors, width), jnp.bfloat16),
            pltpu.VMEM((devices, factors + 8, 2 * factors), jnp.float32),
            pltpu.VMEM((devices - 1, factors + 8, 2 * factors), jnp.float32),
            pltpu.VMEM((cells, width) if devices > 32 else (16, 128), jnp.bfloat16),
            pltpu.SemaphoreType.DMA,
        ]
        + semaphores,
        compiler_params=params(1),
        name="stat_kernel",
    )(h, expression, rel, center)
    count = gram2[factors, factors]
    cross = cross + gram2[factors, :factors][:, None] * center
    mixed = gram2[:factors, factors:]
    gram = (gram2[:factors, :factors] + mixed + mixed.T) / count
    weight = jnp.sum(jnp.where(owner_map == me, atlas_sizes, 0)).astype(jnp.float32) / 65536.0
    gradient = hdot(gram, q) - cross / count
    bound = jnp.max(jnp.sum(gram, axis=1))
    new_specific = jnp.maximum(
        v - (gradient + PENALTY * hdot(gram, v)) / ((1.0 + PENALTY) * bound + 1e-06), 0.0
    )
    share = factors * genes // devices // 8
    terms = jnp.concatenate(
        [
            (weight * gradient).reshape(devices, 8, share),
            jnp.full((devices, 8, 128), weight * bound),
        ],
        axis=2,
    )
    wide = share + 128
    totals = pl.pallas_call(
        functools.partial(sum_kernel, devices),
        out_shape=jax.ShapeDtypeStruct((devices, 8, wide), jnp.float32),
        in_specs=in_vmem(1),
        out_specs=pl.BlockSpec(memory_space=pltpu.VMEM),
        scratch_shapes=[pltpu.VMEM((devices, 8, wide), jnp.float32)] * 3
        + [pltpu.SemaphoreType.DMA((2, stages)), pltpu.SemaphoreType.DMA((2, stages))],
        compiler_params=params(2),
        name="sum_kernel",
    )(terms)
    grad_total = totals[:, :, :share].reshape(factors, genes)
    shared_out = jnp.maximum(shared - grad_total / totals[0, 0, share], 0.0)
    return (h, shared_out, new_specific[None])


def solution(mesh):
    placed = (
        P(("groups", "cells"), None),
        P(("groups", "cells"), None),
        P("groups"),
        P("groups"),
        P(None, ("groups", "cells")),
        P("groups", None),
        P(("groups", "cells"), None, None),
    )
    return jax.shard_map(
        body,
        mesh=mesh,
        in_specs=placed,
        out_specs=(
            P(None, ("groups", "cells")),
            P("groups", None),
            P(("groups", "cells"), None, None),
        ),
        check_vma=False,
    )
```
